32 devices in a mesh: groups: 2 (over x), dates: 16 (over z, y, core).
Axes of the slice: x: 2, y: 2, z: 4, core: 2. Of those that a mesh axis runs over, the one named last changes fastest.
Arguments:
- scenes: bfloat16 [64, 4, 64, 128], P(('groups', 'dates')), parts along dimension 0, may hold values from -10 to 14
- cloud_mask: int32 [64, 64, 128], P(('groups', 'dates')), parts along dimension 0, may hold values 0 or 1
- region: int32 [128, 128], P('groups'), parts along dimension 0, may hold values from 0 to 7
Outputs:
- smoothed: bfloat16 [64, 4, 64, 128], P('groups', None, 'dates'), parts along dimension 0
- similarity: float32 [64, 32], P(('groups', 'dates')), parts along dimension 0
The draws below stay inside these ranges and needn't reach their ends.
There are 2 independent parts, one for each index of `groups`. The reference program is written for one: setup_inputs(seed, part) draws one part's arguments, and reference() takes and returns one part's arrays. A program takes and returns all parts, laid end to end along the dimension named above; each array names one. Nothing has to cross between parts.
All inputs are finite; a program needn't handle non-finite values. No bound on the sum of `cloud_mask` on one device may be relied on, other than what follows from the above.
Results may differ from the reference program's by a relative error of at most 0.0065.
Values may be sent and summed in bfloat16 or wider, within the bound.
A program may use at most 64 MiB of HBM per device.

```python
import jax
import jax.numpy as jnp
from jax import lax

BANDS = 4
COLS = 128
REGIONS = 8
STEPS = 4
DATES = 32
ROWS = 64


def region_map(key):
    return jax.random.randint(jax.random.fold_in(key, 7), (ROWS, COLS), 0, REGIONS).astype(jnp.int32)


def draw_region(key, part):
    return region_map(key)


def draw_scenes(key, part):
    labels = region_map(key)
    offsets = jax.random.uniform(jax.random.fold_in(key, 11), (DATES, BANDS, REGIONS), jnp.float32, 0.5, 3.0)
    base = offsets[:, :, labels]
    noise = jax.random.truncated_normal(jax.random.fold_in(key, 13), -4.0, 4.0, (DATES, BANDS, ROWS, COLS), jnp.float32)
    return (base + noise).astype(jnp.bfloat16)


def plant(result, own_key, low, largest):
    extent = result.shape
    spot = [jax.random.randint(jax.random.fold_in(own_key, axis), (), 0, extent[axis]) for axis in range(len(extent))]
    result = result.at[tuple(spot)].set(low)
    longest = extent.index(max(extent))
    spot[longest] = (spot[longest] + 1) % extent[longest]
    return result.at[tuple(spot)].set(largest)


def setup_inputs(seed: int = 0, part: int = 0) -> dict:
    arg_keys = jax.random.split(jax.random.key(seed), 4)
    part_splits = jax.random.split(jax.random.fold_in(arg_keys[3], part), 4)
    scenes = draw_scenes(jax.random.fold_in(jax.random.fold_in(arg_keys[3], part), 71), part)
    cloud_mask = plant((jax.random.randint(part_splits[1], (DATES, ROWS, COLS), 0, 4) < 3).astype(jnp.int32), jax.random.fold_in(part_splits[1], 1), 0, 1)
    region = draw_region(jax.random.fold_in(jax.random.fold_in(arg_keys[3], part), 71), part)
    return {"scenes": scenes, "cloud_mask": cloud_mask, "region": region}


lam_space = 0.2
lam_time = 0.08


def edge_flux(difference):
    return difference / (1.0 + difference * difference)


def reference(scenes, cloud_mask, region):
    clear = cloud_mask.astype(jnp.float32)
    labels = jnp.arange(REGIONS, dtype=jnp.int32)[:, None, None]
    onehot = (region[None] == labels).astype(jnp.float32)
    counts = jnp.einsum("drc,grc->dg", clear, onehot)
    land_padded = jnp.pad((region > 0).astype(jnp.float32), 1)
    row_weight = land_padded[1:, 1:-1] * land_padded[:-1, 1:-1]
    col_weight = land_padded[1:-1, 1:] * land_padded[1:-1, :-1]
    edges = jnp.arange(DATES + 1, dtype=jnp.int32)
    date_weight = ((edges > 0) & (edges < DATES)).astype(jnp.float32)

    def one_band(band_values):
        values = band_values.astype(jnp.float32)
        sums = jnp.einsum("drc,grc->dg", values * clear, onehot)
        means = sums / (counts + 1.0)
        anomaly = (clear * (values - means[:, region])).astype(jnp.bfloat16)
        current = anomaly.astype(jnp.float32)
        for step_index in range(STEPS):
            padded_rows = jnp.pad(current, ((0, 0), (1, 1), (0, 0)))
            row_flux = lam_space * row_weight * edge_flux(padded_rows[:, 1:] - padded_rows[:, :-1])
            padded_cols = jnp.pad(current, ((0, 0), (0, 0), (1, 1)))
            col_flux = lam_space * col_weight * edge_flux(padded_cols[:, :, 1:] - padded_cols[:, :, :-1])
            padded_dates = jnp.pad(current, ((1, 1), (0, 0), (0, 0)))
            date_flux = lam_time * date_weight[:, None, None] * edge_flux(padded_dates[1:] - padded_dates[:-1])
            current = current + (row_flux[:, 1:] - row_flux[:, :-1]) + (col_flux[:, :, 1:] - col_flux[:, :, :-1]) + (date_flux[1:] - date_flux[:-1])
        return current.astype(jnp.bfloat16)

    smoothed = jnp.moveaxis(lax.map(one_band, jnp.moveaxis(scenes, 1, 0)), 0, 1)
    flat = smoothed.reshape(DATES, -1).astype(jnp.float32)
    similarity = jnp.dot(flat, flat.T, precision=lax.Precision.HIGHEST, preferred_element_type=jnp.float32) / (BANDS * ROWS * COLS)
    return smoothed, similarity
```

```python
import functools

import jax
import jax.numpy as jnp
from jax import lax
from jax.experimental import pallas as pl
from jax.experimental.pallas import tpu as pltpu
from jax.sharding import PartitionSpec as P

REGIONS = 8
STEPS = 4
LANES = 128

lam_space = 0.2
lam_time = 0.08


def edge_flux(difference):
    return difference * pl.reciprocal(1.0 + difference * difference)


def total(values):
    folded = jnp.sum(values.reshape(-1, 8, values.shape[-1]), axis=0)
    return jnp.sum(jnp.sum(folded, axis=0, keepdims=True), axis=1, keepdims=True)


def kernel(
    n,
    scenes_ref, mask_ref, region_ref,
    flat_ref, similarity_ref,
    planes, outgoing, arrived, land, row_weight, col_weight,
    field_a, field_b, final, share, shares,
    send_sem, recv_sem, share_send_sem, share_recv_sem, own_sem,
):
    me = lax.axis_index("dates")
    date_dev, bands, rows, cols = scenes_ref.shape
    rows_dev = rows // n
    window = rows_dev + 2 * STEPS
    group = date_dev * bands
    dates_all = date_dev * n
    pair = 16 // group

    barrier = pltpu.get_barrier_semaphore()

    @pl.loop(1, n)
    def _(k):
        pl.semaphore_signal(barrier, inc=1, device_id={"dates": lax.rem(me + k, n)})

    region = region_ref[...]
    for t in range(date_dev):
        clear = mask_ref[t] > 0
        label = jnp.where(clear, region, -1)
        values = [scenes_ref[t, b].astype(jnp.float32) for b in range(bands)]
        means = [jnp.zeros((rows, cols), jnp.float32) for _ in range(bands)]
        for g in range(REGIONS):
            member = label == g
            scale = 1.0 / (total(jnp.where(member, 1.0, 0.0)) + 1.0)
            for b in range(bands):
                mean = total(jnp.where(member, values[b], 0.0)) * scale
                means[b] = jnp.where(member, mean, means[b])
        for b in range(bands):
            anomaly = jnp.where(clear, values[b] - means[b], 0.0)
            planes[pl.ds(t * bands + b, rows, stride=group), :] = anomaly
    margin = STEPS // pair
    outgoing[:margin] = jnp.zeros((margin, 16, cols), jnp.bfloat16)
    outgoing[margin + rows // pair:] = jnp.zeros((margin, 16, cols), jnp.bfloat16)
    outgoing[margin:margin + rows // pair] = (
        planes[...].reshape(rows // pair, 16, cols).astype(jnp.bfloat16)
    )

    pl.semaphore_wait(barrier, n - 1)

    def block_copy(target):
        return pltpu.make_async_remote_copy(
            src_ref=outgoing.at[pl.ds(target * (rows_dev // pair), window // pair)],
            dst_ref=arrived.at[me],
            send_sem=send_sem.at[target],
            recv_sem=recv_sem.at[me],
            device_id={"dates": target},
        )

    @pl.loop(1, n)
    def _(k):
        block_copy(lax.rem(me + k, n)).start()

    own = pltpu.make_async_copy(
        outgoing.at[pl.ds(me * (rows_dev // pair), window // pair)], arrived.at[me], own_sem
    )
    own.start()

    land[:STEPS, :] = jnp.zeros((STEPS, cols), jnp.float32)
    land[STEPS + rows:, :] = jnp.zeros((STEPS, cols), jnp.float32)
    land[STEPS:STEPS + rows, :] = jnp.where(region > 0, 1.0, 0.0)
    lane = lax.broadcasted_iota(jnp.int32, (8, cols), 1)
    here = [
        jnp.broadcast_to(land[pl.ds(me * rows_dev + r, 1), :], (8, cols)) for r in range(window)
    ]
    for r in range(window):
        after = pltpu.roll(here[r], cols - 1, 1)
        col_weight[r] = jnp.where(lane < cols - 1, lam_space * here[r] * after, 0.0)
        if r + 1 < window:
            row_weight[r] = lam_space * here[r] * here[r + 1]
    share[...] = jnp.zeros(share.shape, jnp.float32)
    field_a[n] = jnp.zeros(field_a.shape[1:], jnp.float32)
    field_b[n] = jnp.zeros(field_b.shape[1:], jnp.float32)

    own.wait()

    def arrival(source):
        return pltpu.make_async_remote_copy(
            src_ref=outgoing.at[pl.ds(0, window // pair)],
            dst_ref=arrived.at[source],
            send_sem=send_sem.at[source],
            recv_sem=recv_sem.at[source],
            device_id={"dates": source},
        )

    @pl.loop(1, n)
    def _(k):
        arrival(lax.rem(me + k, n)).wait_recv()

    @pl.loop(0, n)
    def _(i):
        field_a[i] = arrived[i].astype(jnp.float32).reshape(window, 8, cols)

    upper = lax.broadcasted_iota(jnp.int32, (8, cols), 0) >= bands
    source, target = field_a, field_b
    for step in range(1, STEPS + 1):
        low, high = step, window - step
        count = high - low

        def body(i, before, source=source, target=target, low=low, high=high, step=step, count=count):
            wide = source[i, low - 1:high + 1]
            current = wide[1:-1]
            later = source[i + 1, low:high]
            row_flux = row_weight[low - 1:high] * edge_flux(wide[1:] - wide[:-1])
            right = pltpu.roll(current.reshape(count * 8, cols), cols - 1, 1).reshape(count, 8, cols)
            col_flux = col_weight[low:high] * edge_flux(right - current)
            col_before = pltpu.roll(col_flux.reshape(count * 8, cols), 1, 1).reshape(count, 8, cols)
            following = pltpu.roll(jnp.where(upper, current, later), 4, 1)
            last = jnp.where(i < n - 1, lam_time, 0.0)
            date_flux = jnp.where(upper, last, lam_time) * edge_flux(following - current)
            date_before = pltpu.roll(jnp.where(upper, before, date_flux), 4, 1)
            result = (
                current
                + (row_flux[1:] - row_flux[:-1])
                + (col_flux - col_before)
                + (date_flux - date_before)
            )
            if step < STEPS:
                target[i, low:high] = result
            else:
                for r in range(rows_dev):
                    start = pl.multiple_of((r * n + i) * 8, 8)
                    final[pl.ds(start, 8), :] = result[r]
            return date_flux

        lax.fori_loop(0, n, body, jnp.zeros((count, 8, cols), jnp.float32))
        source, target = target, source

    for b in range(bands):
        for r in range(rows_dev):
            column = (b * rows_dev + r) * cols
            flat_ref[:, column:column + cols] = final[
                pl.ds(r * n * 8 + b, dates_all, stride=bands), :
            ].astype(jnp.bfloat16)
    flat = flat_ref[...]
    product = lax.dot_general(
        flat, flat, (((1,), (1,)), ((), ())), preferred_element_type=jnp.float32
    )
    for j in range(n):
        share[j, :date_dev, :dates_all] = product[j * date_dev:(j + 1) * date_dev]

    def share_copy(target):
        return pltpu.make_async_remote_copy(
            src_ref=share.at[target],
            dst_ref=shares.at[me],
            send_sem=share_send_sem.at[target],
            recv_sem=share_recv_sem.at[me],
            device_id={"dates": target},
        )

    @pl.loop(1, n)
    def _(k):
        share_copy(lax.rem(me + k, n)).start()

    shares[me] = share[me]

    def share_arrival(source):
        return pltpu.make_async_remote_copy(
            src_ref=share.at[source],
            dst_ref=shares.at[source],
            send_sem=share_send_sem.at[source],
            recv_sem=share_recv_sem.at[source],
            device_id={"dates": source},
        )

    @pl.loop(1, n)
    def _(k):
        share_arrival(lax.rem(me + k, n)).wait_recv()

    summed = jnp.sum(shares[...], axis=0) * (1.0 / (bands * rows * cols))
    similarity_ref[...] = summed[:date_dev, :dates_all]

    @pl.loop(1, n)
    def _(k):
        block_copy(lax.rem(me + k, n)).wait_send()
        share_copy(lax.rem(me + k, n)).wait_send()


def local(n, scenes, cloud_mask, region):
    date_dev, bands, rows, cols = scenes.shape
    rows_dev = rows // n
    window = rows_dev + 2 * STEPS
    group = date_dev * bands
    pair = 16 // group
    dates_all = date_dev * n
    wide = max(LANES, dates_all)
    vmem = pl.BlockSpec(memory_space=pltpu.VMEM)
    flat, similarity = pl.pallas_call(
        functools.partial(kernel, n),
        out_shape=(
            jax.ShapeDtypeStruct((dates_all, bands * rows_dev * cols), jnp.bfloat16),
            jax.ShapeDtypeStruct((date_dev, dates_all), jnp.float32),
        ),
        in_specs=[vmem] * 3,
        out_specs=(vmem, vmem),
        scratch_shapes=[
            pltpu.VMEM((rows * group, cols), jnp.float32),
            pltpu.VMEM(((rows + 2 * STEPS) // pair, 16, cols), jnp.bfloat16),
            pltpu.VMEM((n, window // pair, 16, cols), jnp.bfloat16),
            pltpu.VMEM((rows + 2 * STEPS, cols), jnp.float32),
            pltpu.VMEM((window, 8, cols), jnp.float32),
            pltpu.VMEM((window, 8, cols), jnp.float32),
            pltpu.VMEM((n + 1, window, 8, cols), jnp.float32),
            pltpu.VMEM((n + 1, window, 8, cols), jnp.float32),
            pltpu.VMEM((rows_dev * n * 8, cols), jnp.float32),
            pltpu.VMEM((n, 8, wide), jnp.float32),
            pltpu.VMEM((n, 8, wide), jnp.float32),
            pltpu.SemaphoreType.DMA((n,)),
            pltpu.SemaphoreType.DMA((n,)),
            pltpu.SemaphoreType.DMA((n,)),
            pltpu.SemaphoreType.DMA((n,)),
            pltpu.SemaphoreType.DMA,
        ],
        compiler_params=pltpu.CompilerParams(
            collective_id=0, has_side_effects=True, vmem_limit_bytes=44 * 2**20
        ),
    )(scenes, cloud_mask, region)
    return flat.reshape(dates_all, bands, rows_dev, cols), similarity


def solution(mesh):
    in_specs = (
        P(("groups", "dates"), None, None, None),
        P(("groups", "dates"), None, None),
        P("groups", None),
    )
    out_specs = (P("groups", None, "dates", None), P(("groups", "dates"), None))
    return jax.shard_map(
        functools.partial(local, mesh.shape["dates"]),
        mesh=mesh, in_specs=in_specs, out_specs=out_specs, check_vma=False,
    )
```

```python
import functools

import jax
import jax.numpy as jnp
from jax import lax
from jax.experimental import pallas as pl
from jax.experimental.pallas import tpu as pltpu
from jax.sharding import PartitionSpec as P

REGIONS = 8
STEPS = 4
LANES = 128

lam_space = 0.2
lam_time = 0.08


def edge_flux(difference):
    return difference * pl.reciprocal(1.0 + difference * difference, approx=True)


def total(values):
    folded = jnp.sum(values.reshape(-1, 8, values.shape[-1]), axis=0)
    return jnp.sum(jnp.sum(folded, axis=0, keepdims=True), axis=1, keepdims=True)


def kernel(
    n,
    scenes_hbm, mask_hbm, region_hbm,
    flat_ref, similarity_ref,
    scenes_ref, mask_ref, region_ref, planes, outgoing, arrived, land, row_weight, col_weight,
    field_a, field_b, final, share, shares,
    send_sem, recv_sem, share_send_sem, share_recv_sem, own_sem, load_sem,
):
    me = lax.axis_index("dates")
    date_dev, bands, rows, cols = scenes_ref.shape
    rows_dev = rows // n
    window = rows_dev + 2 * STEPS
    group = date_dev * bands
    dates_all = date_dev * n
    pair = 16 // group

    loads = [
        pltpu.make_async_copy(source, target, load_sem.at[i])
        for i, (source, target) in enumerate(
            ((scenes_hbm, scenes_ref), (mask_hbm, mask_ref), (region_hbm, region_ref))
        )
    ]
    for load in loads:
        load.start()
    barrier = pltpu.get_barrier_semaphore()

    @pl.loop(1, n)
    def _(k):
        pl.semaphore_signal(barrier, inc=1, device_id={"dates": lax.rem(me + k, n)})

    for load in loads:
        load.wait()
    region = region_ref[...]
    for t in range(date_dev):
        clear = mask_ref[t] > 0
        label = jnp.where(clear, region, -1)
        values = [scenes_ref[t, b].astype(jnp.float32) for b in range(bands)]
        means = [jnp.zeros((rows, cols), jnp.float32) for _ in range(bands)]
        for g in range(REGIONS):
            member = label == g
            scale = 1.0 / (total(jnp.where(member, 1.0, 0.0)) + 1.0)
            for b in range(bands):
                mean = total(jnp.where(member, values[b], 0.0)) * scale
                means[b] = jnp.where(member, mean, means[b])
        for b in range(bands):
            anomaly = jnp.where(clear, values[b] - means[b], 0.0)
            planes[pl.ds(t * bands + b, rows, stride=group), :] = anomaly
    margin = STEPS // pair
    outgoing[:margin] = jnp.zeros((margin, 16, cols), jnp.bfloat16)
    outgoing[margin + rows // pair:] = jnp.zeros((margin, 16, cols), jnp.bfloat16)
    outgoing[margin:margin + rows // pair] = (
        planes[...].reshape(rows // pair, 16, cols).astype(jnp.bfloat16)
    )

    pl.semaphore_wait(barrier, n - 1)

    def block_copy(target):
        return pltpu.make_async_remote_copy(
            src_ref=outgoing.at[pl.ds(target * (rows_dev // pair), window // pair)],
            dst_ref=arrived.at[me],
            send_sem=send_sem.at[target],
            recv_sem=recv_sem.at[me],
            device_id={"dates": target},
        )

    @pl.loop(1, n)
    def _(k):
        ahead = n // 2 + (k // 2) * (1 - 2 * (k % 2))
        block_copy(lax.rem(me + ahead, n)).start()

    own = pltpu.make_async_copy(
        outgoing.at[pl.ds(me * (rows_dev // pair), window // pair)], arrived.at[me], own_sem
    )
    own.start()

    land[:STEPS, :] = jnp.zeros((STEPS, cols), jnp.float32)
    land[STEPS + rows:, :] = jnp.zeros((STEPS, cols), jnp.float32)
    land[STEPS:STEPS + rows, :] = jnp.where(region > 0, 1.0, 0.0)
    lane = lax.broadcasted_iota(jnp.int32, (8, cols), 1)
    here = [
        jnp.broadcast_to(land[pl.ds(me * rows_dev + r, 1), :], (8, cols)) for r in range(window)
    ]
    for r in range(window):
        after = pltpu.roll(here[r], cols - 1, 1)
        col_weight[r] = jnp.where(lane < cols - 1, lam_space * here[r] * after, 0.0)
        if r + 1 < window:
            row_weight[r] = lam_space * here[r] * here[r + 1]
    share[...] = jnp.zeros(share.shape, jnp.float32)
    field_a[n] = jnp.zeros(field_a.shape[1:], jnp.float32)
    field_b[n] = jnp.zeros(field_b.shape[1:], jnp.float32)

    own.wait()
    field_a[me] = arrived[me].astype(jnp.float32).reshape(window, 8, cols)

    def arrival(source):
        return pltpu.make_async_remote_copy(
            src_ref=outgoing.at[pl.ds(0, window // pair)],
            dst_ref=arrived.at[source],
            send_sem=send_sem.at[source],
            recv_sem=recv_sem.at[source],
            device_id={"dates": source},
        )

    @pl.loop(1, n)
    def _(k):
        i = lax.rem(me + k, n)
        arrival(i).wait_recv()
        field_a[i] = arrived[i].astype(jnp.float32).reshape(window, 8, cols)

    upper = lax.broadcasted_iota(jnp.int32, (8, cols), 0) >= bands
    source, target = field_a, field_b
    for step in range(1, STEPS + 1):
        low, high = step, window - step
        count = high - low

        def body(i, before, source=source, target=target, low=low, high=high, step=step, count=count):
            wide = source[i, low - 1:high + 1]
            current = wide[1:-1]
            later = source[i + 1, low:high]
            row_flux = row_weight[low - 1:high] * edge_flux(wide[1:] - wide[:-1])
            right = pltpu.roll(current.reshape(count * 8, cols), cols - 1, 1).reshape(count, 8, cols)
            col_flux = col_weight[low:high] * edge_flux(right - current)
            col_before = pltpu.roll(col_flux.reshape(count * 8, cols), 1, 1).reshape(count, 8, cols)
            following = pltpu.roll(jnp.where(upper, current, later), 4, 1)
            last = jnp.where(i < n - 1, lam_time, 0.0)
            date_flux = jnp.where(upper, last, lam_time) * edge_flux(following - current)
            date_before = pltpu.roll(jnp.where(upper, before, date_flux), 4, 1)
            result = (
                current
                + (row_flux[1:] - row_flux[:-1])
                + (col_flux - col_before)
                + (date_flux - date_before)
            )
            if step < STEPS:
                target[i, low:high] = result
            else:
                for r in range(rows_dev):
                    start = pl.multiple_of((r * n + i) * 8, 8)
                    final[pl.ds(start, 8), :] = result[r]
            return date_flux

        lax.fori_loop(0, n, body, jnp.zeros((count, 8, cols), jnp.float32))
        source, target = target, source

    for b in range(bands):
        for r in range(rows_dev):
            column = (b * rows_dev + r) * cols
            flat_ref[:, column:column + cols] = final[
                pl.ds(r * n * 8 + b, dates_all, stride=bands), :
            ].astype(jnp.bfloat16)
    flat = flat_ref[...]
    product = lax.dot_general(
        flat, flat, (((1,), (1,)), ((), ())), preferred_element_type=jnp.float32
    )
    for j in range(n):
        share[j, :date_dev, :dates_all] = product[j * date_dev:(j + 1) * date_dev]

    def share_copy(target):
        return pltpu.make_async_remote_copy(
            src_ref=share.at[target],
            dst_ref=shares.at[me],
            send_sem=share_send_sem.at[target],
            recv_sem=share_recv_sem.at[me],
            device_id={"dates": target},
        )

    @pl.loop(1, n)
    def _(k):
        share_copy(lax.rem(me + k, n)).start()

    shares[me] = share[me]

    def share_arrival(source):
        return pltpu.make_async_remote_copy(
            src_ref=share.at[source],
            dst_ref=shares.at[source],
            send_sem=share_send_sem.at[source],
            recv_sem=share_recv_sem.at[source],
            device_id={"dates": source},
        )

    @pl.loop(1, n)
    def _(k):
        share_arrival(lax.rem(me + k, n)).wait_recv()

    summed = jnp.sum(shares[...], axis=0) * (1.0 / (bands * rows * cols))
    similarity_ref[...] = summed[:date_dev, :dates_all]

    @pl.loop(1, n)
    def _(k):
        block_copy(lax.rem(me + k, n)).wait_send()
        share_copy(lax.rem(me + k, n)).wait_send()


def local(n, scenes, cloud_mask, region):
    date_dev, bands, rows, cols = scenes.shape
    rows_dev = rows // n
    window = rows_dev + 2 * STEPS
    group = date_dev * bands
    pair = 16 // group
    dates_all = date_dev * n
    wide = max(LANES, dates_all)
    vmem = pl.BlockSpec(memory_space=pltpu.VMEM)
    flat, similarity = pl.pallas_call(
        functools.partial(kernel, n),
        out_shape=(
            jax.ShapeDtypeStruct((dates_all, bands * rows_dev * cols), jnp.bfloat16),
            jax.ShapeDtypeStruct((date_dev, dates_all), jnp.float32),
        ),
        in_specs=[pl.BlockSpec(memory_space=pltpu.HBM)] * 3,
        out_specs=(vmem, vmem),
        scratch_shapes=[
            pltpu.VMEM(scenes.shape, scenes.dtype),
            pltpu.VMEM(cloud_mask.shape, cloud_mask.dtype),
            pltpu.VMEM(region.shape, region.dtype),
            pltpu.VMEM((rows * group, cols), jnp.float32),
            pltpu.VMEM(((rows + 2 * STEPS) // pair, 16, cols), jnp.bfloat16),
            pltpu.VMEM((n, window // pair, 16, cols), jnp.bfloat16),
            pltpu.VMEM((rows + 2 * STEPS, cols), jnp.float32),
            pltpu.VMEM((window, 8, cols), jnp.float32),
            pltpu.VMEM((window, 8, cols), jnp.float32),
            pltpu.VMEM((n + 1, window, 8, cols), jnp.float32),
            pltpu.VMEM((n + 1, window, 8, cols), jnp.float32),
            pltpu.VMEM((rows_dev * n * 8, cols), jnp.float32),
            pltpu.VMEM((n, 8, wide), jnp.float32),
            pltpu.VMEM((n, 8, wide), jnp.float32),
            pltpu.SemaphoreType.DMA((n,)),
            pltpu.SemaphoreType.DMA((n,)),
            pltpu.SemaphoreType.DMA((n,)),
            pltpu.SemaphoreType.DMA((n,)),
            pltpu.SemaphoreType.DMA,
            pltpu.SemaphoreType.DMA((3,)),
        ],
        compiler_params=pltpu.CompilerParams(
            collective_id=0, has_side_effects=True, vmem_limit_bytes=44 * 2**20
        ),
    )(*(pltpu.with_memory_space_constraint(x, pltpu.HBM) for x in (scenes, cloud_mask, region)))
    return flat.reshape(dates_all, bands, rows_dev, cols), similarity


def solution(mesh):
    in_specs = (
        P(("groups", "dates"), None, None, None),
        P(("groups", "dates"), None, None),
        P("groups", None),
    )
    out_specs = (P("groups", None, "dates", None), P(("groups", "dates"), None))
    return jax.shard_map(
        functools.partial(local, mesh.shape["dates"]),
        mesh=mesh, in_specs=in_specs, out_specs=out_specs, check_vma=False,
    )
```

```python
import functools

import jax
import jax.numpy as jnp
from jax import lax
from jax.experimental import pallas as pl
from jax.experimental.pallas import tpu as pltpu
from jax.sharding import PartitionSpec as P

REGIONS = 8
STEPS = 4
LANES = 128

lam_space = 0.2
lam_time = 0.08


def edge_flux(difference):
    return difference * pl.reciprocal(1.0 + difference * difference, approx=True)


def total(values):
    folded = jnp.sum(values.reshape(-1, 8, values.shape[-1]), axis=0)
    return jnp.sum(jnp.sum(folded, axis=0, keepdims=True), axis=1, keepdims=True)


def kernel(
    n,
    scenes_hbm, mask_hbm, region_hbm,
    flat_ref, similarity_ref,
    scenes_ref, mask_ref, region_ref, planes, outgoing, arrived, land, row_weight, col_weight,
    field_a, field_b, final, share, shares,
    send_sem, recv_sem, share_send_sem, share_recv_sem, own_sem, load_sem,
    pass_send_sem, pass_recv_sem,
):
    me = lax.axis_index("dates")
    date_dev, bands, rows, cols = scenes_ref.shape
    rows_dev = rows // n
    window = rows_dev + 2 * STEPS
    group = date_dev * bands
    dates_all = date_dev * n
    pair = 16 // group

    loads = [
        pltpu.make_async_copy(source, target, load_sem.at[i])
        for i, (source, target) in enumerate(
            ((scenes_hbm, scenes_ref), (mask_hbm, mask_ref), (region_hbm, region_ref))
        )
    ]
    for load in loads:
        load.start()
    barrier = pltpu.get_barrier_semaphore()

    @pl.loop(1, n)
    def _(k):
        pl.semaphore_signal(barrier, inc=1, device_id={"dates": lax.rem(me + k, n)})

    for load in loads:
        load.wait()
    region = region_ref[...]
    for t in range(date_dev):
        clear = mask_ref[t] > 0
        label = jnp.where(clear, region, -1)
        values = [scenes_ref[t, b].astype(jnp.float32) for b in range(bands)]
        means = [jnp.zeros((rows, cols), jnp.float32) for _ in range(bands)]
        for g in range(REGIONS):
            member = label == g
            scale = 1.0 / (total(jnp.where(member, 1.0, 0.0)) + 1.0)
            for b in range(bands):
                mean = total(jnp.where(member, values[b], 0.0)) * scale
                means[b] = jnp.where(member, mean, means[b])
        for b in range(bands):
            anomaly = jnp.where(clear, values[b] - means[b], 0.0)
            planes[pl.ds(t * bands + b, rows, stride=group), :] = anomaly
    margin = STEPS // pair
    outgoing[:margin] = jnp.zeros((margin, 16, cols), jnp.bfloat16)
    outgoing[margin + rows // pair:] = jnp.zeros((margin, 16, cols), jnp.bfloat16)
    outgoing[margin:margin + rows // pair] = (
        planes[...].reshape(rows // pair, 16, cols).astype(jnp.bfloat16)
    )

    pl.semaphore_wait(barrier, n - 1)

    halo, depth = STEPS // pair, rows_dev // pair
    chips, chip, odd = n // 2, me // 2, lax.rem(me, 2)
    partner = me + 1 - 2 * odd

    def ahead(k):
        return chips // 2 + (k // 2) * (1 - 2 * lax.rem(k, 2))

    def block_copy(target, core):
        return pltpu.make_async_remote_copy(
            src_ref=outgoing.at[pl.ds(target * depth + core * halo, depth + halo)],
            dst_ref=arrived.at[me, pl.ds(core * halo, depth + halo)],
            send_sem=send_sem.at[target],
            recv_sem=recv_sem.at[me],
            device_id={"dates": target},
        )

    def partner_copy():
        return pltpu.make_async_remote_copy(
            src_ref=outgoing.at[pl.ds(partner * depth, window // pair)],
            dst_ref=arrived.at[me],
            send_sem=send_sem.at[partner],
            recv_sem=recv_sem.at[me],
            device_id={"dates": partner},
        )

    @pl.loop(1, chips)
    def _(k):
        other = lax.rem(chip + ahead(k), chips)
        for core in range(2):
            block_copy(2 * other + core, core).start()

    partner_copy().start()

    own = pltpu.make_async_copy(
        outgoing.at[pl.ds(me * (rows_dev // pair), window // pair)], arrived.at[me], own_sem
    )
    own.start()

    land[:STEPS, :] = jnp.zeros((STEPS, cols), jnp.float32)
    land[STEPS + rows:, :] = jnp.zeros((STEPS, cols), jnp.float32)
    land[STEPS:STEPS + rows, :] = jnp.where(region > 0, 1.0, 0.0)
    lane = lax.broadcasted_iota(jnp.int32, (8, cols), 1)
    here = [
        jnp.broadcast_to(land[pl.ds(me * rows_dev + r, 1), :], (8, cols)) for r in range(window)
    ]
    for r in range(window):
        after = pltpu.roll(here[r], cols - 1, 1)
        col_weight[r] = jnp.where(lane < cols - 1, lam_space * here[r] * after, 0.0)
        if r + 1 < window:
            row_weight[r] = lam_space * here[r] * here[r + 1]
    share[...] = jnp.zeros(share.shape, jnp.float32)
    field_a[n] = jnp.zeros(field_a.shape[1:], jnp.float32)
    field_b[n] = jnp.zeros(field_b.shape[1:], jnp.float32)

    own.wait()
    field_a[me] = arrived[me].astype(jnp.float32).reshape(window, 8, cols)

    def arrival(source):
        return pltpu.make_async_remote_copy(
            src_ref=outgoing.at[pl.ds(0, depth + halo)],
            dst_ref=arrived.at[source, pl.ds(odd * halo, depth + halo)],
            send_sem=send_sem.at[source],
            recv_sem=recv_sem.at[source],
            device_id={"dates": source},
        )

    def pass_on(source):
        return pltpu.make_async_remote_copy(
            src_ref=arrived.at[source, pl.ds(depth + odd * (halo - depth), halo)],
            dst_ref=arrived.at[source, pl.ds(odd * (depth + halo), halo)],
            send_sem=pass_send_sem.at[source],
            recv_sem=pass_recv_sem.at[source],
            device_id={"dates": partner},
        )

    def passed(source):
        return pltpu.make_async_remote_copy(
            src_ref=outgoing.at[pl.ds(0, halo)],
            dst_ref=arrived.at[source, pl.ds((1 - odd) * (depth + halo), halo)],
            send_sem=pass_send_sem.at[source],
            recv_sem=pass_recv_sem.at[source],
            device_id={"dates": partner},
        )

    @pl.loop(1, chips)
    def _(k):
        other = lax.rem(chip + chips - ahead(k), chips)
        for core in range(2):
            arrival(2 * other + core).wait_recv()
            pass_on(2 * other + core).start()

    pltpu.make_async_remote_copy(
        src_ref=outgoing.at[pl.ds(0, window // pair)],
        dst_ref=arrived.at[partner],
        send_sem=send_sem.at[partner],
        recv_sem=recv_sem.at[partner],
        device_id={"dates": partner},
    ).wait_recv()
    field_a[partner] = arrived[partner].astype(jnp.float32).reshape(window, 8, cols)

    @pl.loop(1, chips)
    def _(k):
        other = lax.rem(chip + chips - ahead(k), chips)
        for core in range(2):
            i = 2 * other + core
            passed(i).wait_recv()
            field_a[i] = arrived[i].astype(jnp.float32).reshape(window, 8, cols)

    upper = lax.broadcasted_iota(jnp.int32, (8, cols), 0) >= bands
    source, target = field_a, field_b
    for step in range(1, STEPS + 1):
        low, high = step, window - step
        count = high - low

        def body(i, before, source=source, target=target, low=low, high=high, step=step, count=count):
            wide = source[i, low - 1:high + 1]
            current = wide[1:-1]
            later = source[i + 1, low:high]
            row_flux = row_weight[low - 1:high] * edge_flux(wide[1:] - wide[:-1])
            right = pltpu.roll(current.reshape(count * 8, cols), cols - 1, 1).reshape(count, 8, cols)
            col_flux = col_weight[low:high] * edge_flux(right - current)
            col_before = pltpu.roll(col_flux.reshape(count * 8, cols), 1, 1).reshape(count, 8, cols)
            following = pltpu.roll(jnp.where(upper, current, later), 4, 1)
            last = jnp.where(i < n - 1, lam_time, 0.0)
            date_flux = jnp.where(upper, last, lam_time) * edge_flux(following - current)
            date_before = pltpu.roll(jnp.where(upper, before, date_flux), 4, 1)
            result = (
                current
                + (row_flux[1:] - row_flux[:-1])
                + (col_flux - col_before)
                + (date_flux - date_before)
            )
            if step < STEPS:
                target[i, low:high] = result
            else:
                for r in range(rows_dev):
                    start = pl.multiple_of((r * n + i) * 8, 8)
                    final[pl.ds(start, 8), :] = result[r]
            return date_flux

        lax.fori_loop(0, n, body, jnp.zeros((count, 8, cols), jnp.float32))
        source, target = target, source

    for b in range(bands):
        for r in range(rows_dev):
            column = (b * rows_dev + r) * cols
            flat_ref[:, column:column + cols] = final[
                pl.ds(r * n * 8 + b, dates_all, stride=bands), :
            ].astype(jnp.bfloat16)
    flat = flat_ref[...]
    product = lax.dot_general(
        flat, flat, (((1,), (1,)), ((), ())), preferred_element_type=jnp.float32
    )
    for j in range(n):
        share[j, :date_dev, :dates_all] = product[j * date_dev:(j + 1) * date_dev]

    def share_copy(target):
        return pltpu.make_async_remote_copy(
            src_ref=share.at[target],
            dst_ref=shares.at[me],
            send_sem=share_send_sem.at[target],
            recv_sem=share_recv_sem.at[me],
            device_id={"dates": target},
        )

    @pl.loop(1, n)
    def _(k):
        share_copy(lax.rem(me + k, n)).start()

    shares[me] = share[me]

    def share_arrival(source):
        return pltpu.make_async_remote_copy(
            src_ref=share.at[source],
            dst_ref=shares.at[source],
            send_sem=share_send_sem.at[source],
            recv_sem=share_recv_sem.at[source],
            device_id={"dates": source},
        )

    @pl.loop(1, n)
    def _(k):
        share_arrival(lax.rem(me + k, n)).wait_recv()

    summed = jnp.sum(shares[...], axis=0) * (1.0 / (bands * rows * cols))
    similarity_ref[...] = summed[:date_dev, :dates_all]

    @pl.loop(1, n)
    def _(k):
        share_copy(lax.rem(me + k, n)).wait_send()

    @pl.loop(1, chips)
    def _(k):
        other = lax.rem(chip + k, chips)
        for core in range(2):
            block_copy(2 * other + core, core).wait_send()
            pass_on(2 * other + core).wait_send()

    partner_copy().wait_send()


def local(n, scenes, cloud_mask, region):
    date_dev, bands, rows, cols = scenes.shape
    rows_dev = rows // n
    window = rows_dev + 2 * STEPS
    group = date_dev * bands
    pair = 16 // group
    dates_all = date_dev * n
    wide = max(LANES, dates_all)
    vmem = pl.BlockSpec(memory_space=pltpu.VMEM)
    flat, similarity = pl.pallas_call(
        functools.partial(kernel, n),
        out_shape=(
            jax.ShapeDtypeStruct((dates_all, bands * rows_dev * cols), jnp.bfloat16),
            jax.ShapeDtypeStruct((date_dev, dates_all), jnp.float32),
        ),
        in_specs=[pl.BlockSpec(memory_space=pltpu.HBM)] * 3,
        out_specs=(vmem, vmem),
        scratch_shapes=[
            pltpu.VMEM(scenes.shape, scenes.dtype),
            pltpu.VMEM(cloud_mask.shape, cloud_mask.dtype),
            pltpu.VMEM(region.shape, region.dtype),
            pltpu.VMEM((rows * group, cols), jnp.float32),
            pltpu.VMEM(((rows + 2 * STEPS) // pair, 16, cols), jnp.bfloat16),
            pltpu.VMEM((n, window // pair, 16, cols), jnp.bfloat16),
            pltpu.VMEM((rows + 2 * STEPS, cols), jnp.float32),
            pltpu.VMEM((window, 8, cols), jnp.float32),
            pltpu.VMEM((window, 8, cols), jnp.float32),
            pltpu.VMEM((n + 1, window, 8, cols), jnp.float32),
            pltpu.VMEM((n + 1, window, 8, cols), jnp.float32),
            pltpu.VMEM((rows_dev * n * 8, cols), jnp.float32),
            pltpu.VMEM((n, 8, wide), jnp.float32),
            pltpu.VMEM((n, 8, wide), jnp.float32),
            pltpu.SemaphoreType.DMA((n,)),
            pltpu.SemaphoreType.DMA((n,)),
            pltpu.SemaphoreType.DMA((n,)),
            pltpu.SemaphoreType.DMA((n,)),
            pltpu.SemaphoreType.DMA,
            pltpu.SemaphoreType.DMA((3,)),
            pltpu.SemaphoreType.DMA((n,)),
            pltpu.SemaphoreType.DMA((n,)),
        ],
        compiler_params=pltpu.CompilerParams(
            collective_id=0, has_side_effects=True, vmem_limit_bytes=44 * 2**20
        ),
    )(*(pltpu.with_memory_space_constraint(x, pltpu.HBM) for x in (scenes, cloud_mask, region)))
    return flat.reshape(dates_all, bands, rows_dev, cols), similarity


def solution(mesh):
    in_specs = (
        P(("groups", "dates"), None, None, None),
        P(("groups", "dates"), None, None),
        P("groups", None),
    )
    out_specs = (P("groups", None, "dates", None), P(("groups", "dates"), None))
    return jax.shard_map(
        functools.partial(local, mesh.shape["dates"]),
        mesh=mesh, in_specs=in_specs, out_specs=out_specs, check_vma=False,
    )
```

```python
import functools

import jax
import jax.numpy as jnp
from jax import lax
from jax.experimental import pallas as pl
from jax.experimental.pallas import tpu as pltpu
from jax.sharding import PartitionSpec as P

REGIONS = 8
STEPS = 4
LANES = 128

lam_space = 0.2
lam_time = 0.08


def edge_flux(difference):
    return difference * pl.reciprocal(1.0 + difference * difference, approx=True)


def totals(planes):
    folded = [jnp.sum(plane.reshape(-1, 8, plane.shape[-1]), axis=0) for plane in planes]
    return jnp.sum(jnp.sum(jnp.stack(folded), axis=1), axis=1, keepdims=True)


def kernel(
    n,
    scenes_hbm, mask_hbm, region_hbm,
    flat_ref, similarity_ref,
    scenes_ref, mask_ref, region_ref, planes, outgoing, arrived, land, row_weight, col_weight,
    field_a, field_b, final, share, shares,
    send_sem, recv_sem, share_send_sem, share_recv_sem, own_sem, load_sem,
    pass_send_sem, pass_recv_sem,
):
    me = lax.axis_index("dates")
    date_dev, bands, rows, cols = scenes_ref.shape
    rows_dev = rows // n
    window = rows_dev + 2 * STEPS
    group = date_dev * bands
    dates_all = date_dev * n
    pair = 16 // group

    loads = [
        pltpu.make_async_copy(source, target, load_sem.at[i])
        for i, (source, target) in enumerate(
            ((scenes_hbm, scenes_ref), (mask_hbm, mask_ref), (region_hbm, region_ref))
        )
    ]
    for load in loads:
        load.start()
    barrier = pltpu.get_barrier_semaphore()

    @pl.loop(1, n)
    def _(k):
        pl.semaphore_signal(barrier, inc=1, device_id={"dates": lax.rem(me + k, n)})

    for load in loads:
        load.wait()
    region = region_ref[...]
    for t in range(date_dev):
        clear = mask_ref[t] > 0
        label = jnp.where(clear, region, -1)
        values = [scenes_ref[t, b].astype(jnp.float32) for b in range(bands)]
        counts = totals([jnp.where(label == g, 1.0, 0.0) for g in range(REGIONS)])
        means = []
        for b in range(bands):
            sums = totals([jnp.where(label == g, values[b], 0.0) for g in range(REGIONS)])
            table = jnp.broadcast_to(sums / (counts + 1.0), (REGIONS, cols))
            mean = jnp.zeros((rows, cols), jnp.float32)
            for g in range(REGIONS):
                mean = jnp.where(label == g, table[g:g + 1], mean)
            means.append(mean)
        for b in range(bands):
            anomaly = jnp.where(clear, values[b] - means[b], 0.0)
            planes[pl.ds(t * bands + b, rows, stride=group), :] = anomaly
    margin = STEPS // pair
    outgoing[:margin] = jnp.zeros((margin, 16, cols), jnp.bfloat16)
    outgoing[margin + rows // pair:] = jnp.zeros((margin, 16, cols), jnp.bfloat16)
    outgoing[margin:margin + rows // pair] = (
        planes[...].reshape(rows // pair, 16, cols).astype(jnp.bfloat16)
    )

    pl.semaphore_wait(barrier, n - 1)

    halo, depth = STEPS // pair, rows_dev // pair
    chips, chip, odd = n // 2, me // 2, lax.rem(me, 2)
    partner = me + 1 - 2 * odd

    def ahead(k):
        return chips // 2 + (k // 2) * (1 - 2 * lax.rem(k, 2))

    def block_copy(target, core):
        return pltpu.make_async_remote_copy(
            src_ref=outgoing.at[pl.ds(target * depth + core * halo, depth + halo)],
            dst_ref=arrived.at[me, pl.ds(core * halo, depth + halo)],
            send_sem=send_sem.at[target],
            recv_sem=recv_sem.at[me],
            device_id={"dates": target},
        )

    def partner_copy():
        return pltpu.make_async_remote_copy(
            src_ref=outgoing.at[pl.ds(partner * depth, window // pair)],
            dst_ref=arrived.at[me],
            send_sem=send_sem.at[partner],
            recv_sem=recv_sem.at[me],
            device_id={"dates": partner},
        )

    @pl.loop(1, chips)
    def _(k):
        other = lax.rem(chip + ahead(k), chips)
        for core in range(2):
            block_copy(2 * other + core, core).start()

    partner_copy().start()

    own = pltpu.make_async_copy(
        outgoing.at[pl.ds(me * (rows_dev // pair), window // pair)], arrived.at[me], own_sem
    )
    own.start()

    land[:STEPS, :] = jnp.zeros((STEPS, cols), jnp.float32)
    land[STEPS + rows:, :] = jnp.zeros((STEPS, cols), jnp.float32)
    land[STEPS:STEPS + rows, :] = jnp.where(region > 0, 1.0, 0.0)
    lane = lax.broadcasted_iota(jnp.int32, (8, cols), 1)
    here = [
        jnp.broadcast_to(land[pl.ds(me * rows_dev + r, 1), :], (8, cols)) for r in range(window)
    ]
    for r in range(window):
        after = pltpu.roll(here[r], cols - 1, 1)
        col_weight[r] = jnp.where(lane < cols - 1, lam_space * here[r] * after, 0.0)
        if r + 1 < window:
            row_weight[r] = lam_space * here[r] * here[r + 1]
    share[...] = jnp.zeros(share.shape, jnp.float32)
    field_a[n] = jnp.zeros(field_a.shape[1:], jnp.float32)
    field_b[n] = jnp.zeros(field_b.shape[1:], jnp.float32)

    own.wait()
    field_a[me] = arrived[me].astype(jnp.float32).reshape(window, 8, cols)

    def arrival(source):
        return pltpu.make_async_remote_copy(
            src_ref=outgoing.at[pl.ds(0, depth + halo)],
            dst_ref=arrived.at[source, pl.ds(odd * halo, depth + halo)],
            send_sem=send_sem.at[source],
            recv_sem=recv_sem.at[source],
            device_id={"dates": source},
        )

    def pass_on(source):
        return pltpu.make_async_remote_copy(
            src_ref=arrived.at[source, pl.ds(depth + odd * (halo - depth), halo)],
            dst_ref=arrived.at[source, pl.ds(odd * (depth + halo), halo)],
            send_sem=pass_send_sem.at[source],
            recv_sem=pass_recv_sem.at[source],
            device_id={"dates": partner},
        )

    def passed(source):
        return pltpu.make_async_remote_copy(
            src_ref=outgoing.at[pl.ds(0, halo)],
            dst_ref=arrived.at[source, pl.ds((1 - odd) * (depth + halo), halo)],
            send_sem=pass_send_sem.at[source],
            recv_sem=pass_recv_sem.at[source],
            device_id={"dates": partner},
        )

    @pl.loop(1, chips)
    def _(k):
        other = lax.rem(chip + chips - ahead(k), chips)
        for core in range(2):
            arrival(2 * other + core).wait_recv()
            pass_on(2 * other + core).start()

    pltpu.make_async_remote_copy(
        src_ref=outgoing.at[pl.ds(0, window // pair)],
        dst_ref=arrived.at[partner],
        send_sem=send_sem.at[partner],
        recv_sem=recv_sem.at[partner],
        device_id={"dates": partner},
    ).wait_recv()
    field_a[partner] = arrived[partner].astype(jnp.float32).reshape(window, 8, cols)

    @pl.loop(1, chips)
    def _(k):
        other = lax.rem(chip + chips - ahead(k), chips)
        for core in range(2):
            i = 2 * other + core
            passed(i).wait_recv()
            field_a[i] = arrived[i].astype(jnp.float32).reshape(window, 8, cols)

    upper = lax.broadcasted_iota(jnp.int32, (8, cols), 0) >= bands
    source, target = field_a, field_b
    for step in range(1, STEPS + 1):
        low, high = step, window - step
        count = high - low

        def body(i, before, source=source, target=target, low=low, high=high, step=step, count=count):
            wide = source[i, low - 1:high + 1]
            current = wide[1:-1]
            later = source[i + 1, low:high]
            row_flux = row_weight[low - 1:high] * edge_flux(wide[1:] - wide[:-1])
            right = pltpu.roll(current.reshape(count * 8, cols), cols - 1, 1).reshape(count, 8, cols)
            col_flux = col_weight[low:high] * edge_flux(right - current)
            col_before = pltpu.roll(col_flux.reshape(count * 8, cols), 1, 1).reshape(count, 8, cols)
            following = pltpu.roll(jnp.where(upper, current, later), 4, 1)
            last = jnp.where(i < n - 1, lam_time, 0.0)
            date_flux = jnp.where(upper, last, lam_time) * edge_flux(following - current)
            date_before = pltpu.roll(jnp.where(upper, before, date_flux), 4, 1)
            result = (
                current
                + (row_flux[1:] - row_flux[:-1])
                + (col_flux - col_before)
                + (date_flux - date_before)
            )
            if step < STEPS:
                target[i, low:high] = result
            else:
                for r in range(rows_dev):
                    start = pl.multiple_of((r * n + i) * 8, 8)
                    final[pl.ds(start, 8), :] = result[r]
            return date_flux

        lax.fori_loop(0, n, body, jnp.zeros((count, 8, cols), jnp.float32))
        source, target = target, source

    for b in range(bands):
        for r in range(rows_dev):
            column = (b * rows_dev + r) * cols
            flat_ref[:, column:column + cols] = final[
                pl.ds(r * n * 8 + b, dates_all, stride=bands), :
            ].astype(jnp.bfloat16)
    flat = flat_ref[...]
    product = lax.dot_general(
        flat, flat, (((1,), (1,)), ((), ())), preferred_element_type=jnp.float32
    )
    for j in range(n):
        share[j, :date_dev, :dates_all] = product[j * date_dev:(j + 1) * date_dev]

    def share_copy(target):
        return pltpu.make_async_remote_copy(
            src_ref=share.at[target],
            dst_ref=shares.at[me],
            send_sem=share_send_sem.at[target],
            recv_sem=share_recv_sem.at[me],
            device_id={"dates": target},
        )

    @pl.loop(1, n)
    def _(k):
        share_copy(lax.rem(me + k, n)).start()

    shares[me] = share[me]

    def share_arrival(source):
        return pltpu.make_async_remote_copy(
            src_ref=share.at[source],
            dst_ref=shares.at[source],
            send_sem=share_send_sem.at[source],
            recv_sem=share_recv_sem.at[source],
            device_id={"dates": source},
        )

    @pl.loop(1, n)
    def _(k):
        share_arrival(lax.rem(me + k, n)).wait_recv()

    summed = jnp.sum(shares[...], axis=0) * (1.0 / (bands * rows * cols))
    similarity_ref[...] = summed[:date_dev, :dates_all]

    @pl.loop(1, n)
    def _(k):
        share_copy(lax.rem(me + k, n)).wait_send()

    @pl.loop(1, chips)
    def _(k):
        other = lax.rem(chip + k, chips)
        for core in range(2):
            block_copy(2 * other + core, core).wait_send()
            pass_on(2 * other + core).wait_send()

    partner_copy().wait_send()


def local(n, scenes, cloud_mask, region):
    date_dev, bands, rows, cols = scenes.shape
    rows_dev = rows // n
    window = rows_dev + 2 * STEPS
    group = date_dev * bands
    pair = 16 // group
    dates_all = date_dev * n
    wide = max(LANES, dates_all)
    vmem = pl.BlockSpec(memory_space=pltpu.VMEM)
    flat, similarity = pl.pallas_call(
        functools.partial(kernel, n),
        out_shape=(
            jax.ShapeDtypeStruct((dates_all, bands * rows_dev * cols), jnp.bfloat16),
            jax.ShapeDtypeStruct((date_dev, dates_all), jnp.float32),
        ),
        in_specs=[pl.BlockSpec(memory_space=pltpu.HBM)] * 3,
        out_specs=(vmem, vmem),
        scratch_shapes=[
            pltpu.VMEM(scenes.shape, scenes.dtype),
            pltpu.VMEM(cloud_mask.shape, cloud_mask.dtype),
            pltpu.VMEM(region.shape, region.dtype),
            pltpu.VMEM((rows * group, cols), jnp.float32),
            pltpu.VMEM(((rows + 2 * STEPS) // pair, 16, cols), jnp.bfloat16),
            pltpu.VMEM((n, window // pair, 16, cols), jnp.bfloat16),
            pltpu.VMEM((rows + 2 * STEPS, cols), jnp.float32),
            pltpu.VMEM((window, 8, cols), jnp.float32),
            pltpu.VMEM((window, 8, cols), jnp.float32),
            pltpu.VMEM((n + 1, window, 8, cols), jnp.float32),
            pltpu.VMEM((n + 1, window, 8, cols), jnp.float32),
            pltpu.VMEM((rows_dev * n * 8, cols), jnp.float32),
            pltpu.VMEM((n, 8, wide), jnp.float32),
            pltpu.VMEM((n, 8, wide), jnp.float32),
            pltpu.SemaphoreType.DMA((n,)),
            pltpu.SemaphoreType.DMA((n,)),
            pltpu.SemaphoreType.DMA((n,)),
            pltpu.SemaphoreType.DMA((n,)),
            pltpu.SemaphoreType.DMA,
            pltpu.SemaphoreType.DMA((3,)),
            pltpu.SemaphoreType.DMA((n,)),
            pltpu.SemaphoreType.DMA((n,)),
        ],
        compiler_params=pltpu.CompilerParams(
            collective_id=0, has_side_effects=True, vmem_limit_bytes=44 * 2**20
        ),
    )(*(pltpu.with_memory_space_constraint(x, pltpu.HBM) for x in (scenes, cloud_mask, region)))
    return flat.reshape(dates_all, bands, rows_dev, cols), similarity


def solution(mesh):
    in_specs = (
        P(("groups", "dates"), None, None, None),
        P(("groups", "dates"), None, None),
        P("groups", None),
    )
    out_specs = (P("groups", None, "dates", None), P(("groups", "dates"), None))
    return jax.shard_map(
        functools.partial(local, mesh.shape["dates"]),
        mesh=mesh, in_specs=in_specs, out_specs=out_specs, check_vma=False,
    )
```

```python
import functools

import jax
import jax.numpy as jnp
from jax import lax
from jax.experimental import pallas as pl
from jax.experimental.pallas import tpu as pltpu
from jax.sharding import PartitionSpec as P

REGIONS = 8
STEPS = 4
LANES = 128

lam_space = 0.2
lam_time = 0.08


def edge_flux(difference):
    return difference * pl.reciprocal(1.0 + difference * difference, approx=True)


def total(values):
    folded = jnp.sum(values.reshape(-1, 8, values.shape[-1]), axis=0)
    return jnp.sum(jnp.sum(folded, axis=0, keepdims=True), axis=1, keepdims=True)


def kernel(
    n,
    scenes_hbm, mask_hbm, region_hbm,
    flat_ref, similarity_ref,
    scenes_ref, mask_ref, region_ref, planes, outgoing, arrived, land, row_weight, col_weight,
    field_a, field_b, final, share, shares,
    send_sem, recv_sem, share_send_sem, share_recv_sem, own_sem, load_sem,
    pass_send_sem, pass_recv_sem,
):
    me = lax.axis_index("dates")
    date_dev, bands, rows, cols = scenes_ref.shape
    rows_dev = rows // n
    window = rows_dev + 2 * STEPS
    group = date_dev * bands
    dates_all = date_dev * n
    pair = 16 // group

    loads = [
        pltpu.make_async_copy(source, target, load_sem.at[i])
        for i, (source, target) in enumerate(
            ((scenes_hbm, scenes_ref), (mask_hbm, mask_ref), (region_hbm, region_ref))
        )
    ]
    for load in loads:
        load.start()
    barrier = pltpu.get_barrier_semaphore()

    @pl.loop(1, n)
    def _(k):
        pl.semaphore_signal(barrier, inc=1, device_id={"dates": lax.rem(me + k, n)})

    for load in loads:
        load.wait()
    region = region_ref[...]
    for t in range(date_dev):
        clear = mask_ref[t] > 0
        label = jnp.where(clear, region, -1)
        values = [scenes_ref[t, b].astype(jnp.float32) for b in range(bands)]
        means = [jnp.zeros((rows, cols), jnp.float32) for _ in range(bands)]
        for g in range(REGIONS):
            member = label == g
            scale = 1.0 / (total(jnp.where(member, 1.0, 0.0)) + 1.0)
            for b in range(bands):
                mean = total(jnp.where(member, values[b], 0.0)) * scale
                means[b] = jnp.where(member, mean, means[b])
        for b in range(bands):
            anomaly = jnp.where(clear, values[b] - means[b], 0.0)
            planes[pl.ds(t * bands + b, rows, stride=group), :] = anomaly
    margin = STEPS // pair
    outgoing[:margin] = jnp.zeros((margin, 16, cols), jnp.bfloat16)
    outgoing[margin + rows // pair:] = jnp.zeros((margin, 16, cols), jnp.bfloat16)
    outgoing[margin:margin + rows // pair] = (
        planes[...].reshape(rows // pair, 16, cols).astype(jnp.bfloat16)
    )

    pl.semaphore_wait(barrier, n - 1)

    halo, depth = STEPS // pair, rows_dev // pair
    chips, chip, odd = n // 2, me // 2, lax.rem(me, 2)
    partner = me + 1 - 2 * odd

    def ahead(k):
        return chips // 2 + (k // 2) * (1 - 2 * lax.rem(k, 2))

    def block_copy(target, core):
        return pltpu.make_async_remote_copy(
            src_ref=outgoing.at[pl.ds(target * depth + core * halo, depth + halo)],
            dst_ref=arrived.at[me, pl.ds(core * halo, depth + halo)],
            send_sem=send_sem.at[target],
            recv_sem=recv_sem.at[me],
            device_id={"dates": target},
        )

    def partner_copy():
        return pltpu.make_async_remote_copy(
            src_ref=outgoing.at[pl.ds(partner * depth, window // pair)],
            dst_ref=arrived.at[me],
            send_sem=send_sem.at[partner],
            recv_sem=recv_sem.at[me],
            device_id={"dates": partner},
        )

    @pl.loop(1, chips)
    def _(k):
        other = lax.rem(chip + ahead(k), chips)
        for core in range(2):
            block_copy(2 * other + core, core).start()

    partner_copy().start()

    own = pltpu.make_async_copy(
        outgoing.at[pl.ds(me * (rows_dev // pair), window // pair)], arrived.at[me], own_sem
    )
    own.start()

    land[:STEPS, :] = jnp.zeros((STEPS, cols), jnp.float32)
    land[STEPS + rows:, :] = jnp.zeros((STEPS, cols), jnp.float32)
    land[STEPS:STEPS + rows, :] = jnp.where(region > 0, 1.0, 0.0)
    lane = lax.broadcasted_iota(jnp.int32, (8, cols), 1)
    here = [
        jnp.broadcast_to(land[pl.ds(me * rows_dev + r, 1), :], (8, cols)) for r in range(window)
    ]
    for r in range(window):
        after = pltpu.roll(here[r], cols - 1, 1)
        col_weight[r] = jnp.where(lane < cols - 1, lam_space * here[r] * after, 0.0)
        if r + 1 < window:
            row_weight[r] = lam_space * here[r] * here[r + 1]
    share[...] = jnp.zeros(share.shape, jnp.float32)
    field_a[n] = jnp.zeros(field_a.shape[1:], jnp.float32)
    field_b[n] = jnp.zeros(field_b.shape[1:], jnp.float32)

    own.wait()
    field_a[me] = arrived[me].astype(jnp.float32).reshape(window, 8, cols)

    def arrival(source):
        return pltpu.make_async_remote_copy(
            src_ref=outgoing.at[pl.ds(0, depth + halo)],
            dst_ref=arrived.at[source, pl.ds(odd * halo, depth + halo)],
            send_sem=send_sem.at[source],
            recv_sem=recv_sem.at[source],
            device_id={"dates": source},
        )

    def pass_on(source):
        return pltpu.make_async_remote_copy(
            src_ref=arrived.at[source, pl.ds(depth + odd * (halo - depth), halo)],
            dst_ref=arrived.at[source, pl.ds(odd * (depth + halo), halo)],
            send_sem=pass_send_sem.at[source],
            recv_sem=pass_recv_sem.at[source],
            device_id={"dates": partner},
        )

    def passed(source):
        return pltpu.make_async_remote_copy(
            src_ref=outgoing.at[pl.ds(0, halo)],
            dst_ref=arrived.at[source, pl.ds((1 - odd) * (depth + halo), halo)],
            send_sem=pass_send_sem.at[source],
            recv_sem=pass_recv_sem.at[source],
            device_id={"dates": partner},
        )

    @pl.loop(1, chips)
    def _(k):
        other = lax.rem(chip + chips - ahead(k), chips)
        for core in range(2):
            arrival(2 * other + core).wait_recv()
            pass_on(2 * other + core).start()

    pltpu.make_async_remote_copy(
        src_ref=outgoing.at[pl.ds(0, window // pair)],
        dst_ref=arrived.at[partner],
        send_sem=send_sem.at[partner],
        recv_sem=recv_sem.at[partner],
        device_id={"dates": partner},
    ).wait_recv()
    field_a[partner] = arrived[partner].astype(jnp.float32).reshape(window, 8, cols)

    @pl.loop(1, chips)
    def _(k):
        other = lax.rem(chip + chips - ahead(k), chips)
        for core in range(2):
            i = 2 * other + core
            passed(i).wait_recv()
            field_a[i] = arrived[i].astype(jnp.float32).reshape(window, 8, cols)

    upper = lax.broadcasted_iota(jnp.int32, (8, cols), 0) >= bands
    source, target = field_a, field_b
    for step in range(1, STEPS + 1):
        low, high = step, window - step
        count = high - low

        def body(i, before, source=source, target=target, low=low, high=high, step=step, count=count):
            wide = source[i, low - 1:high + 1]
            current = wide[1:-1]
            later = source[i + 1, low:high]
            row_flux = row_weight[low - 1:high] * edge_flux(wide[1:] - wide[:-1])
            right = pltpu.roll(current.reshape(count * 8, cols), cols - 1, 1).reshape(count, 8, cols)
            col_flux = col_weight[low:high] * edge_flux(right - current)
            col_before = pltpu.roll(col_flux.reshape(count * 8, cols), 1, 1).reshape(count, 8, cols)
            following = pltpu.roll(jnp.where(upper, current, later), 4, 1)
            last = jnp.where(i < n - 1, lam_time, 0.0)
            date_flux = jnp.where(upper, last, lam_time) * edge_flux(following - current)
            date_before = pltpu.roll(jnp.where(upper, before, date_flux), 4, 1)
            result = (
                current
                + (row_flux[1:] - row_flux[:-1])
                + (col_flux - col_before)
                + (date_flux - date_before)
            )
            if step < STEPS:
                target[i, low:high] = result
            else:
                for r in range(rows_dev):
                    start = pl.multiple_of((r * n + i) * 8, 8)
                    final[pl.ds(start, 8), :] = result[r]
            return date_flux

        lax.fori_loop(0, n, body, jnp.zeros((count, 8, cols), jnp.float32), unroll=2)
        source, target = target, source

    for b in range(bands):
        for r in range(rows_dev):
            column = (b * rows_dev + r) * cols
            flat_ref[:, column:column + cols] = final[
                pl.ds(r * n * 8 + b, dates_all, stride=bands), :
            ].astype(jnp.bfloat16)
    flat = flat_ref[...]
    product = lax.dot_general(
        flat, flat, (((1,), (1,)), ((), ())), preferred_element_type=jnp.float32
    )
    for j in range(n):
        share[j, :date_dev, :dates_all] = product[j * date_dev:(j + 1) * date_dev]

    def share_copy(target):
        return pltpu.make_async_remote_copy(
            src_ref=share.at[target],
            dst_ref=shares.at[me],
            send_sem=share_send_sem.at[target],
            recv_sem=share_recv_sem.at[me],
            device_id={"dates": target},
        )

    @pl.loop(1, n)
    def _(k):
        share_copy(lax.rem(me + k, n)).start()

    shares[me] = share[me]

    def share_arrival(source):
        return pltpu.make_async_remote_copy(
            src_ref=share.at[source],
            dst_ref=shares.at[source],
            send_sem=share_send_sem.at[source],
            recv_sem=share_recv_sem.at[source],
            device_id={"dates": source},
        )

    @pl.loop(1, n)
    def _(k):
        share_arrival(lax.rem(me + k, n)).wait_recv()

    summed = jnp.sum(shares[...], axis=0) * (1.0 / (bands * rows * cols))
    similarity_ref[...] = summed[:date_dev, :dates_all]

    @pl.loop(1, n)
    def _(k):
        share_copy(lax.rem(me + k, n)).wait_send()

    @pl.loop(1, chips)
    def _(k):
        other = lax.rem(chip + k, chips)
        for core in range(2):
            block_copy(2 * other + core, core).wait_send()
            pass_on(2 * other + core).wait_send()

    partner_copy().wait_send()


def local(n, scenes, cloud_mask, region):
    date_dev, bands, rows, cols = scenes.shape
    rows_dev = rows // n
    window = rows_dev + 2 * STEPS
    group = date_dev * bands
    pair = 16 // group
    dates_all = date_dev * n
    wide = max(LANES, dates_all)
    vmem = pl.BlockSpec(memory_space=pltpu.VMEM)
    flat, similarity = pl.pallas_call(
        functools.partial(kernel, n),
        out_shape=(
            jax.ShapeDtypeStruct((dates_all, bands * rows_dev * cols), jnp.bfloat16),
            jax.ShapeDtypeStruct((date_dev, dates_all), jnp.float32),
        ),
        in_specs=[pl.BlockSpec(memory_space=pltpu.HBM)] * 3,
        out_specs=(vmem, vmem),
        scratch_shapes=[
            pltpu.VMEM(scenes.shape, scenes.dtype),
            pltpu.VMEM(cloud_mask.shape, cloud_mask.dtype),
            pltpu.VMEM(region.shape, region.dtype),
            pltpu.VMEM((rows * group, cols), jnp.float32),
            pltpu.VMEM(((rows + 2 * STEPS) // pair, 16, cols), jnp.bfloat16),
            pltpu.VMEM((n, window // pair, 16, cols), jnp.bfloat16),
            pltpu.VMEM((rows + 2 * STEPS, cols), jnp.float32),
            pltpu.VMEM((window, 8, cols), jnp.float32),
            pltpu.VMEM((window, 8, cols), jnp.float32),
            pltpu.VMEM((n + 1, window, 8, cols), jnp.float32),
            pltpu.VMEM((n + 1, window, 8, cols), jnp.float32),
            pltpu.VMEM((rows_dev * n * 8, cols), jnp.float32),
            pltpu.VMEM((n, 8, wide), jnp.float32),
            pltpu.VMEM((n, 8, wide), jnp.float32),
            pltpu.SemaphoreType.DMA((n,)),
            pltpu.SemaphoreType.DMA((n,)),
            pltpu.SemaphoreType.DMA((n,)),
            pltpu.SemaphoreType.DMA((n,)),
            pltpu.SemaphoreType.DMA,
            pltpu.SemaphoreType.DMA((3,)),
            pltpu.SemaphoreType.DMA((n,)),
            pltpu.SemaphoreType.DMA((n,)),
        ],
        compiler_params=pltpu.CompilerParams(
            collective_id=0, has_side_effects=True, vmem_limit_bytes=44 * 2**20
        ),
    )(*(pltpu.with_memory_space_constraint(x, pltpu.HBM) for x in (scenes, cloud_mask, region)))
    return flat.reshape(dates_all, bands, rows_dev, cols), similarity


def solution(mesh):
    in_specs = (
        P(("groups", "dates"), None, None, None),
        P(("groups", "dates"), None, None),
        P("groups", None),
    )
    out_specs = (P("groups", None, "dates", None), P(("groups", "dates"), None))
    return jax.shard_map(
        functools.partial(local, mesh.shape["dates"]),
        mesh=mesh, in_specs=in_specs, out_specs=out_specs, check_vma=False,
    )
```

```python
import functools

import jax
import jax.numpy as jnp
from jax import lax
from jax.experimental import pallas as pl
from jax.experimental.pallas import tpu as pltpu
from jax.sharding import PartitionSpec as P

REGIONS = 8
STEPS = 4
LANES = 128

lam_space = 0.2
lam_time = 0.08


def edge_flux(difference):
    return difference * pl.reciprocal(1.0 + difference * difference, approx=True)


def total(values):
    folded = jnp.sum(values.reshape(-1, 8, values.shape[-1]), axis=0)
    return jnp.sum(jnp.sum(folded, axis=0, keepdims=True), axis=1, keepdims=True)


def kernel(
    n,
    scenes_hbm, mask_hbm, region_hbm,
    flat_ref, similarity_ref,
    scenes_ref, mask_ref, region_ref, planes, outgoing, arrived, land, row_weight, col_weight,
    field_a, field_b, final, share, shares,
    send_sem, recv_sem, share_send_sem, share_recv_sem, own_sem, load_sem,
    pass_send_sem, pass_recv_sem,
):
    me = lax.axis_index("dates")
    date_dev, bands, rows, cols = scenes_ref.shape
    rows_dev = rows // n
    window = rows_dev + 2 * STEPS
    group = date_dev * bands
    dates_all = date_dev * n
    pair = 16 // group

    loads = [
        pltpu.make_async_copy(source, target, load_sem.at[i])
        for i, (source, target) in enumerate(
            ((scenes_hbm, scenes_ref), (mask_hbm, mask_ref), (region_hbm, region_ref))
        )
    ]
    for load in loads:
        load.start()
    barrier = pltpu.get_barrier_semaphore()

    @pl.loop(1, n)
    def _(k):
        pl.semaphore_signal(barrier, inc=1, device_id={"dates": lax.rem(me + k, n)})

    for load in loads:
        load.wait()
    region = region_ref[...]
    for t in range(date_dev):
        clear = mask_ref[t] > 0
        label = jnp.where(clear, region, -1)
        values = [scenes_ref[t, b].astype(jnp.float32) for b in range(bands)]
        means = [jnp.zeros((rows, cols), jnp.float32) for _ in range(bands)]
        for g in range(REGIONS):
            member = label == g
            scale = 1.0 / (total(jnp.where(member, 1.0, 0.0)) + 1.0)
            for b in range(bands):
                mean = total(jnp.where(member, values[b], 0.0)) * scale
                means[b] = jnp.where(member, mean, means[b])
        for b in range(bands):
            anomaly = jnp.where(clear, values[b] - means[b], 0.0)
            planes[pl.ds(t * bands + b, rows, stride=group), :] = anomaly
    margin = STEPS // pair
    outgoing[:margin] = jnp.zeros((margin, 16, cols), jnp.bfloat16)
    outgoing[margin + rows // pair:] = jnp.zeros((margin, 16, cols), jnp.bfloat16)
    outgoing[margin:margin + rows // pair] = (
        planes[...].reshape(rows // pair, 16, cols).astype(jnp.bfloat16)
    )

    pl.semaphore_wait(barrier, n - 1)

    halo, depth = STEPS // pair, rows_dev // pair
    chips, chip, odd = n // 2, me // 2, lax.rem(me, 2)
    partner = me + 1 - 2 * odd

    def ahead(k):
        return chips // 2 + (k // 2) * (1 - 2 * lax.rem(k, 2))

    def block_copy(target, core):
        return pltpu.make_async_remote_copy(
            src_ref=outgoing.at[pl.ds(target * depth + core * halo, depth + halo)],
            dst_ref=arrived.at[me, pl.ds(core * halo, depth + halo)],
            send_sem=send_sem.at[target],
            recv_sem=recv_sem.at[me],
            device_id={"dates": target},
        )

    def partner_copy():
        return pltpu.make_async_remote_copy(
            src_ref=outgoing.at[pl.ds(partner * depth, window // pair)],
            dst_ref=arrived.at[me],
            send_sem=send_sem.at[partner],
            recv_sem=recv_sem.at[me],
            device_id={"dates": partner},
        )

    @pl.loop(1, chips)
    def _(k):
        other = lax.rem(chip + ahead(k), chips)
        for core in range(2):
            block_copy(2 * other + core, core).start()

    partner_copy().start()

    own = pltpu.make_async_copy(
        outgoing.at[pl.ds(me * (rows_dev // pair), window // pair)], arrived.at[me], own_sem
    )
    own.start()

    land[:STEPS, :] = jnp.zeros((STEPS, cols), jnp.float32)
    land[STEPS + rows:, :] = jnp.zeros((STEPS, cols), jnp.float32)
    land[STEPS:STEPS + rows, :] = jnp.where(region > 0, 1.0, 0.0)
    lane = lax.broadcasted_iota(jnp.int32, (8, cols), 1)
    here = [
        jnp.broadcast_to(land[pl.ds(me * rows_dev + r, 1), :], (8, cols)) for r in range(window)
    ]
    for r in range(window):
        after = pltpu.roll(here[r], cols - 1, 1)
        col_weight[r] = jnp.where(lane < cols - 1, lam_space * here[r] * after, 0.0)
        if r + 1 < window:
            row_weight[r] = lam_space * here[r] * here[r + 1]
    share[...] = jnp.zeros(share.shape, jnp.float32)
    field_a[n] = jnp.zeros(field_a.shape[1:], jnp.float32)
    field_b[n] = jnp.zeros(field_b.shape[1:], jnp.float32)

    own.wait()
    field_a[me] = arrived[me].astype(jnp.float32).reshape(window, 8, cols)

    def arrival(source):
        return pltpu.make_async_remote_copy(
            src_ref=outgoing.at[pl.ds(0, depth + halo)],
            dst_ref=arrived.at[source, pl.ds(odd * halo, depth + halo)],
            send_sem=send_sem.at[source],
            recv_sem=recv_sem.at[source],
            device_id={"dates": source},
        )

    def pass_on(source):
        return pltpu.make_async_remote_copy(
            src_ref=arrived.at[source, pl.ds(depth + odd * (halo - depth), halo)],
            dst_ref=arrived.at[source, pl.ds(odd * (depth + halo), halo)],
            send_sem=pass_send_sem.at[source],
            recv_sem=pass_recv_sem.at[source],
            device_id={"dates": partner},
        )

    def passed(source):
        return pltpu.make_async_remote_copy(
            src_ref=outgoing.at[pl.ds(0, halo)],
            dst_ref=arrived.at[source, pl.ds((1 - odd) * (depth + halo), halo)],
            send_sem=pass_send_sem.at[source],
            recv_sem=pass_recv_sem.at[source],
            device_id={"dates": partner},
        )

    @pl.loop(1, chips)
    def _(k):
        other = lax.rem(chip + chips - ahead(k), chips)
        for core in range(2):
            arrival(2 * other + core).wait_recv()
            pass_on(2 * other + core).start()

    pltpu.make_async_remote_copy(
        src_ref=outgoing.at[pl.ds(0, window // pair)],
        dst_ref=arrived.at[partner],
        send_sem=send_sem.at[partner],
        recv_sem=recv_sem.at[partner],
        device_id={"dates": partner},
    ).wait_recv()
    field_a[partner] = arrived[partner].astype(jnp.float32).reshape(window, 8, cols)

    @pl.loop(1, chips)
    def _(k):
        other = lax.rem(chip + chips - ahead(k), chips)
        for core in range(2):
            i = 2 * other + core
            passed(i).wait_recv()
            field_a[i] = arrived[i].astype(jnp.float32).reshape(window, 8, cols)

    upper = lax.broadcasted_iota(jnp.int32, (8, cols), 0) >= bands
    source, target = field_a, field_b
    for step in range(1, STEPS + 1):
        low, high = step, window - step
        count = high - low

        def body(i, before, source=source, target=target, low=low, high=high, step=step, count=count):
            wide = source[i, low - 1:high + 1]
            current = wide[1:-1]
            later = source[i + 1, low:high]
            row_flux = row_weight[low - 1:high] * edge_flux(wide[1:] - wide[:-1])
            right = pltpu.roll(current.reshape(count * 8, cols), cols - 1, 1).reshape(count, 8, cols)
            col_flux = col_weight[low:high] * edge_flux(right - current)
            col_before = pltpu.roll(col_flux.reshape(count * 8, cols), 1, 1).reshape(count, 8, cols)
            following = pltpu.roll(jnp.where(upper, current, later), 4, 1)
            last = jnp.where(i < n - 1, lam_time, 0.0)
            date_flux = jnp.where(upper, last, lam_time) * edge_flux(following - current)
            date_before = pltpu.roll(jnp.where(upper, before, date_flux), 4, 1)
            result = (
                current
                + (row_flux[1:] - row_flux[:-1])
                + (col_flux - col_before)
                + (date_flux - date_before)
            )
            if step < STEPS:
                target[i, low:high] = result
            else:
                for r in range(rows_dev):
                    start = pl.multiple_of((r * n + i) * 8, 8)
                    final[pl.ds(start, 8), :] = result[r]
            return date_flux

        lax.fori_loop(0, n, body, jnp.zeros((count, 8, cols), jnp.float32), unroll=4)
        source, target = target, source

    for b in range(bands):
        for r in range(rows_dev):
            column = (b * rows_dev + r) * cols
            flat_ref[:, column:column + cols] = final[
                pl.ds(r * n * 8 + b, dates_all, stride=bands), :
            ].astype(jnp.bfloat16)
    flat = flat_ref[...]
    product = lax.dot_general(
        flat, flat, (((1,), (1,)), ((), ())), preferred_element_type=jnp.float32
    )
    for j in range(n):
        share[j, :date_dev, :dates_all] = product[j * date_dev:(j + 1) * date_dev]

    def share_copy(target):
        return pltpu.make_async_remote_copy(
            src_ref=share.at[target],
            dst_ref=shares.at[me],
            send_sem=share_send_sem.at[target],
            recv_sem=share_recv_sem.at[me],
            device_id={"dates": target},
        )

    @pl.loop(1, n)
    def _(k):
        share_copy(lax.rem(me + k, n)).start()

    shares[me] = share[me]

    def share_arrival(source):
        return pltpu.make_async_remote_copy(
            src_ref=share.at[source],
            dst_ref=shares.at[source],
            send_sem=share_send_sem.at[source],
            recv_sem=share_recv_sem.at[source],
            device_id={"dates": source},
        )

    @pl.loop(1, n)
    def _(k):
        share_arrival(lax.rem(me + k, n)).wait_recv()

    summed = jnp.sum(shares[...], axis=0) * (1.0 / (bands * rows * cols))
    similarity_ref[...] = summed[:date_dev, :dates_all]

    @pl.loop(1, n)
    def _(k):
        share_copy(lax.rem(me + k, n)).wait_send()

    @pl.loop(1, chips)
    def _(k):
        other = lax.rem(chip + k, chips)
        for core in range(2):
            block_copy(2 * other + core, core).wait_send()
            pass_on(2 * other + core).wait_send()

    partner_copy().wait_send()


def local(n, scenes, cloud_mask, region):
    date_dev, bands, rows, cols = scenes.shape
    rows_dev = rows // n
    window = rows_dev + 2 * STEPS
    group = date_dev * bands
    pair = 16 // group
    dates_all = date_dev * n
    wide = max(LANES, dates_all)
    vmem = pl.BlockSpec(memory_space=pltpu.VMEM)
    flat, similarity = pl.pallas_call(
        functools.partial(kernel, n),
        out_shape=(
            jax.ShapeDtypeStruct((dates_all, bands * rows_dev * cols), jnp.bfloat16),
            jax.ShapeDtypeStruct((date_dev, dates_all), jnp.float32),
        ),
        in_specs=[pl.BlockSpec(memory_space=pltpu.HBM)] * 3,
        out_specs=(vmem, vmem),
        scratch_shapes=[
            pltpu.VMEM(scenes.shape, scenes.dtype),
            pltpu.VMEM(cloud_mask.shape, cloud_mask.dtype),
            pltpu.VMEM(region.shape, region.dtype),
            pltpu.VMEM((rows * group, cols), jnp.float32),
            pltpu.VMEM(((rows + 2 * STEPS) // pair, 16, cols), jnp.bfloat16),
            pltpu.VMEM((n, window // pair, 16, cols), jnp.bfloat16),
            pltpu.VMEM((rows + 2 * STEPS, cols), jnp.float32),
            pltpu.VMEM((window, 8, cols), jnp.float32),
            pltpu.VMEM((window, 8, cols), jnp.float32),
            pltpu.VMEM((n + 1, window, 8, cols), jnp.float32),
            pltpu.VMEM((n + 1, window, 8, cols), jnp.float32),
            pltpu.VMEM((rows_dev * n * 8, cols), jnp.float32),
            pltpu.VMEM((n, 8, wide), jnp.float32),
            pltpu.VMEM((n, 8, wide), jnp.float32),
            pltpu.SemaphoreType.DMA((n,)),
            pltpu.SemaphoreType.DMA((n,)),
            pltpu.SemaphoreType.DMA((n,)),
            pltpu.SemaphoreType.DMA((n,)),
            pltpu.SemaphoreType.DMA,
            pltpu.SemaphoreType.DMA((3,)),
            pltpu.SemaphoreType.DMA((n,)),
            pltpu.SemaphoreType.DMA((n,)),
        ],
        compiler_params=pltpu.CompilerParams(
            collective_id=0, has_side_effects=True, vmem_limit_bytes=44 * 2**20
        ),
    )(*(pltpu.with_memory_space_constraint(x, pltpu.HBM) for x in (scenes, cloud_mask, region)))
    return flat.reshape(dates_all, bands, rows_dev, cols), similarity


def solution(mesh):
    in_specs = (
        P(("groups", "dates"), None, None, None),
        P(("groups", "dates"), None, None),
        P("groups", None),
    )
    out_specs = (P("groups", None, "dates", None), P(("groups", "dates"), None))
    return jax.shard_map(
        functools.partial(local, mesh.shape["dates"]),
        mesh=mesh, in_specs=in_specs, out_specs=out_specs, check_vma=False,
    )
```
